32 devices in a mesh: group: 2 (over x), attn: 8 (over z, y), expert: 2 (over core).
Axes of the slice: x: 2, y: 2, z: 4, core: 2. Of those that a mesh axis runs over, the one named last changes fastest.
Arguments:
- queries: bfloat16 [256, 6144], P(('group', 'attn'), 'expert'), parts along dimension 0, may hold values from -6 to 6
- new_kv: bfloat16 [256, 2, 1024], P(('group', 'attn'), None, 'expert'), parts along dimension 0, may hold values from -6 to 6
- cache_kv: bfloat16 [256, 2, 16, 1024], P(('group', 'attn'), None, None, 'expert'), parts along dimension 0, may hold values from -6 to 6
- lengths: int32 [256], P(('group', 'attn')), parts along dimension 0, may hold values from 1 to 16, as said below
- residual: bfloat16 [256, 6144], P(('group', 'attn'), 'expert'), parts along dimension 0, may hold values from -12 to 12
- norm_gain: bfloat16 [6144], replicated, may hold values from 0.099609375 to 1.8984375
- expert_ids: int32 [256, 2], P(('group', 'attn')), parts along dimension 0, may hold values from 0 to 3, all different within a row; in each aligned block of 16 rows (0 to 15, 16 to 31, ...) at most 12 rows name the same one
- route_weights: bfloat16 [256, 2], P(('group', 'attn')), parts along dimension 0, may hold values from 0.19921875 to 1
- w_up: bfloat16 [6144, 32768], P(None, ('attn', 'expert')), may hold values from -0.078125 to 0.078125
- w_down: bfloat16 [32768, 6144], P(('attn', 'expert')), may hold values from -0.0625 to 0.0625
Outputs:
- layer_out: bfloat16 [256, 6144], P(('group', 'attn'), 'expert'), parts along dimension 0
The draws below stay inside these ranges and needn't reach their ends.
There are 2 independent parts, one for each index of `group`. The reference program is written for one: setup_inputs(seed, part) draws one part's arguments, and reference() takes and returns one part's arrays. A program takes and returns all parts, laid end to end along the dimension named above; an argument that names none is the same for every part. Nothing has to cross between parts.
Inputs may be any that keep to these rules, and one draw needn't show every extreme that they name: Request t holds valid cache entries at positions 0 to lengths[t] - 1; in every draw some request holds all 16. `expert_ids`: each token names 2 different experts. Among the 16 tokens of one device's rows no expert is named more than 12 times, and in every draw some expert is named exactly 12 times in some device's rows.
All inputs are finite; a program needn't handle non-finite values.
Results may differ from the reference program's by a relative error of at most 0.012.
Values may be sent and summed in bfloat16 or wider, within the bound.
A program may use at most 128 MiB of HBM per device.

```python
import math
import jax
import jax.numpy as jnp
import numpy as np
from jax import lax

D = 6144
KV_HEADS = 8
HEAD_DIM = 128
EXPERTS = 4
FF = 8192
TOPK = 2
TOK_DEV = 16
LEN = 16
CAP = 12
TOKENS = 128


def draw_queries(key, part):
    key = jax.random.fold_in(key, 11)
    values = jax.random.normal(key, (TOKENS, D), jnp.float32)
    return jnp.clip(values, -6.0, 6.0).astype(jnp.bfloat16)


def draw_new_kv(key, part):
    key = jax.random.fold_in(key, 12)
    values = jax.random.normal(key, (TOKENS, 2, KV_HEADS * HEAD_DIM), jnp.float32)
    return jnp.clip(values, -6.0, 6.0).astype(jnp.bfloat16)


def draw_cache_kv(key, part):
    key = jax.random.fold_in(key, 13)
    values = jax.random.normal(key, (TOKENS, 2, LEN, KV_HEADS * HEAD_DIM), jnp.float32)
    return jnp.clip(values, -6.0, 6.0).astype(jnp.bfloat16)


def draw_lengths(key, part):
    key = jax.random.fold_in(key, 14)
    first, second = jax.random.split(key)
    counts = jax.random.randint(first, (TOKENS,), 1, LEN + 1)
    full_at = jax.random.randint(second, (), 0, TOKENS)
    return counts.at[full_at].set(LEN).astype(jnp.int32)


def draw_residual(key, part):
    key = jax.random.fold_in(key, 15)
    first, second, third = jax.random.split(key, 3)
    row_scale = jnp.exp(jax.random.uniform(first, (TOKENS, 1), jnp.float32, -1.15, 1.15))
    col_scale = jnp.exp(jax.random.uniform(second, (1, D), jnp.float32, -1.15, 1.15))
    values = jax.random.normal(third, (TOKENS, D), jnp.float32)
    return jnp.clip(0.25 * values * row_scale * col_scale, -12.0, 12.0).astype(jnp.bfloat16)


def level_of(key, dims, cuts, least, top_value):
    level = 1.0
    for dim, shards_of in cuts:
        draws = jax.random.uniform(jax.random.fold_in(jax.random.fold_in(key, 6), dim), (shards_of,), jnp.float32, least / len(cuts), top_value / len(cuts))
        level = level * jnp.repeat(jnp.exp(draws), dims[dim] // shards_of).reshape((-1,) + (1,) * (len(dims) - 1 - dim))
    return level


def deal_out(key, own, number, rows, number_of, top, reach, skew):
    sequence = jax.random.permutation(key, number_of)
    crowded, usual = load_shares(number_of, rows * top, reach, skew, True), load_shares(number_of, rows * top, reach, skew, False)
    places = jnp.arange(number_of)

    def named(sizes, offset_by):
        used = int((sizes > 0).sum())
        fixed = max(1, used // 4)
        moved = fixed + (places - fixed + offset_by * (used - fixed)) % max(1, number_of - fixed)
        return jnp.zeros((number_of,), jnp.int32).at[sequence[jnp.where(places < fixed, places, moved)]].set(jnp.asarray(sizes, jnp.int32))

    sizes = jnp.where(number % 4 == 0, named(crowded, number // 4), named(usual, number - number // 4 - 1))
    mixed = jax.random.permutation(jax.random.fold_in(own, 3), number_of)
    source_of, sink = mixed[0:number_of // 2 * 2:2], mixed[1:number_of // 2 * 2:2]
    margin = jnp.minimum(sizes[source_of] - 1, reach - sizes[sink]) // 2
    margin = jnp.where((source_of == sequence[0]) | (sink == sequence[0]) | (sizes[sink] == 0), 0, jnp.maximum(margin, 0))
    moved = jax.random.randint(jax.random.fold_in(own, 4), (number_of // 2,), 0, 1 << 20) % (margin + 1)
    sizes = sizes.at[source_of].add(-moved).at[sink].add(moved)
    members = jnp.searchsorted(jnp.cumsum(sizes), jnp.arange(rows * top), side="right").astype(jnp.int32)
    listing = members.reshape(top, rows).T
    listing = listing[jax.random.permutation(jax.random.fold_in(own, 1), rows)]
    offset_by = jax.random.randint(jax.random.fold_in(own, 2), (rows, 1), 0, top)
    return jnp.take_along_axis(listing, (jnp.arange(top)[None, :] + offset_by) % top, axis=1)


def load_shares(number_of, total, most, lean, full):
    loads = [(1 << 20) // math.isqrt(standing ** lean) + 1 for standing in range(1, number_of + 1)]
    largest = most if full else min(most, max(-(-total // number_of), total * loads[0] // sum(loads)))
    least = 1 if total - largest >= number_of - 1 else 0
    given, rest = [largest] + [least] * (number_of - 1), total - largest - least * (number_of - 1)
    while rest > 0:
        free = [i for i in range(1, number_of) if given[i] < largest] or [i for i in range(1, number_of) if given[i] < most]
        whole, budget = sum([loads[i] for i in free]), rest
        for i in free:
            addition = min(most - given[i], max(1, budget * loads[i] // whole), rest)
            given[i] = given[i] + addition
            rest = rest - addition
    return np.array(given)


def centred(own_key, extent, deviation, most, cuts=(), dtype=jnp.bfloat16):
    result = jax.random.normal(own_key, extent, jnp.float32) * deviation
    if len(cuts) > 0:
        result = level_of(own_key, extent, cuts, -0.22, 0.18) * result
    return jnp.clip(result, min=-most, max=most).astype(dtype)


def setup_inputs(seed: int = 0, part: int = 0) -> dict:
    splits = jax.random.split(jax.random.key(seed), 11)
    part_keys = jax.random.split(jax.random.fold_in(splits[10], part), 11)
    queries = draw_queries(jax.random.fold_in(jax.random.fold_in(splits[10], part), 71), part)
    new_kv = draw_new_kv(jax.random.fold_in(jax.random.fold_in(splits[10], part), 71), part)
    cache_kv = draw_cache_kv(jax.random.fold_in(jax.random.fold_in(splits[10], part), 71), part)
    lengths = draw_lengths(jax.random.fold_in(jax.random.fold_in(splits[10], part), 71), part)
    residual = draw_residual(jax.random.fold_in(jax.random.fold_in(splits[10], part), 71), part)
    norm_gain = jnp.clip(1.0 + 0.18 * jax.random.normal(splits[5], (D,), jnp.float32), 0.099609375, 1.8984375).astype(jnp.bfloat16)
    expert_ids_keys = jax.random.split(jax.random.fold_in(part_keys[6], 1), TOKENS // TOK_DEV)
    expert_ids_turns = jax.random.permutation(jax.random.fold_in(part_keys[6], 3), TOKENS // TOK_DEV)
    expert_ids = jax.vmap(lambda own, number: deal_out(jax.random.fold_in(part_keys[6], 2), own, number, TOK_DEV, EXPERTS, TOPK, CAP, 1))(expert_ids_keys, expert_ids_turns).reshape((TOKENS, TOPK))
    route_weights = jnp.clip(0.19921875 + 0.80078125 * jax.random.uniform(part_keys[7], (TOKENS, TOPK), jnp.float32) ** level_of(part_keys[7], (TOKENS, TOPK), ((0, 8),), -0.2, 0.2), 0.19921875, 1.0).astype(jnp.bfloat16)
    w_up = centred(splits[8], (D, EXPERTS * FF), D ** -0.5, 0.078125, ((1, 16),))
    w_down = centred(splits[9], (EXPERTS * FF, D), FF ** -0.5, 0.0625, ((0, 16),))
    return dict(queries=queries, new_kv=new_kv, cache_kv=cache_kv, lengths=lengths, residual=residual, norm_gain=norm_gain, expert_ids=expert_ids, route_weights=route_weights, w_up=w_up, w_down=w_down)


EPSILON = 1e-05
NEG_FILL = -1e+30

def attend(queries, new_kv, cache_kv, lengths):
    tok_rows = queries.shape[0]
    kv_heads = new_kv.shape[-1] // HEAD_DIM
    group_size = queries.shape[1] // (kv_heads * HEAD_DIM)
    cache_len = cache_kv.shape[2]
    scaling = HEAD_DIM ** (-0.5)
    query_vec = queries.astype(jnp.float32).reshape(tok_rows, kv_heads, group_size, HEAD_DIM)
    key_cache = cache_kv[:, 0].astype(jnp.float32).reshape(tok_rows, cache_len, kv_heads, HEAD_DIM)
    value_cache = cache_kv[:, 1].astype(jnp.float32).reshape(tok_rows, cache_len, kv_heads, HEAD_DIM)
    new_key = new_kv[:, 0].astype(jnp.float32).reshape(tok_rows, kv_heads, HEAD_DIM)
    new_value = new_kv[:, 1].astype(jnp.float32).reshape(tok_rows, kv_heads, HEAD_DIM)
    visible = (jnp.arange(cache_len)[None, :] < lengths[:, None])[:, None, None, :]
    old_scores = jnp.einsum('tkgd,tskd->tkgs', query_vec, key_cache) * scaling
    old_scores = jnp.where(visible, old_scores, NEG_FILL)
    new_scores = jnp.einsum('tkgd,tkd->tkg', query_vec, new_key) * scaling
    row_max = jnp.maximum(lax.optimization_barrier(jnp.max(old_scores, axis=-1)), new_scores)
    old_probs = jnp.where(visible, jnp.exp(old_scores - row_max[..., None]), 0.0)
    new_probs = jnp.exp(new_scores - row_max)
    totals = lax.optimization_barrier(jnp.sum(old_probs, axis=-1)) + new_probs
    old_weight = lax.optimization_barrier((old_probs / totals[..., None]).astype(jnp.bfloat16)).astype(jnp.float32)
    new_weight = lax.optimization_barrier((new_probs / totals).astype(jnp.bfloat16)).astype(jnp.float32)
    attended = jnp.einsum('tkgs,tskd->tkgd', old_weight, value_cache) + new_weight[..., None] * new_value[:, :, None, :]
    return attended.reshape(tok_rows, -1).astype(jnp.bfloat16)

def normalize(stream_rows, norm_gain):
    widened = stream_rows.astype(jnp.float32)
    mean_square = lax.optimization_barrier(jnp.mean(widened * widened, axis=-1, keepdims=True))
    return (widened * lax.rsqrt(mean_square + EPSILON) * norm_gain.astype(jnp.float32)).astype(jnp.bfloat16)

def reference(queries, new_kv, cache_kv, lengths, residual, norm_gain, expert_ids, route_weights, w_up, w_down):
    attended = attend(queries, new_kv, cache_kv, lengths)
    stream = (residual.astype(jnp.float32) + attended.astype(jnp.float32)).astype(jnp.bfloat16)
    normed = normalize(stream, norm_gain)
    mixture = jnp.zeros((stream.shape[0], stream.shape[1]), jnp.float32)
    for expert in range(EXPERTS):
        up_proj = jnp.dot(normed, w_up[:, expert * FF:(expert + 1) * FF], preferred_element_type=jnp.float32)
        hidden = jax.nn.silu(up_proj).astype(jnp.bfloat16)
        output = jnp.dot(hidden, w_down[expert * FF:(expert + 1) * FF, :], preferred_element_type=jnp.float32)
        weighting = lax.optimization_barrier(jnp.sum(jnp.where(expert_ids == expert, route_weights.astype(jnp.float32), 0.0), axis=1))
        mixture = mixture + weighting[:, None] * output
    return (stream.astype(jnp.float32) + mixture).astype(jnp.bfloat16)
```

```python
import functools

import jax
import jax.numpy as jnp
from jax import lax
from jax.experimental import pallas as pl
from jax.experimental.pallas import tpu as pltpu
from jax.sharding import PartitionSpec as P

HEAD_DIM = 128
EXPERTS = 4
EPSILON = 1e-05
NEG_FILL = -1e30
MESH = pl.DeviceIdType.MESH
CHUNKS = 4
PIECES = 8
F32 = jnp.float32
BF16 = jnp.bfloat16


def kernel(
    m, q_ref, nkv_ref, cache_ref, res_ref, gain_ref, meta_ref, wu_hbm, wd_hbm, out_ref,
    wu, wd, x, normed, hidden, core_out, core_in, keep, mem_out, mem_in, exp_out, exp_in,
    wu_sem, wd_sem, x_recv, e_send, m_send, c_send,
    co_send, co_recv, mo_send, mo_recv, eo_send, eo_recv,
):
    a = lax.axis_index("attn")
    c = lax.axis_index("expert")
    e = lax.div(a, m)
    j = lax.rem(a, m)
    core = {"attn": a, "expert": 1 - c}
    rows, half = q_ref.shape
    width = half // CHUNKS

    def expert_at(k):
        return lax.rem(e + k, EXPERTS)

    def member_at(k):
        return lax.rem(j + k, m)

    def device(ee, jj):
        return {"attn": ee * m + jj, "expert": c}

    peers = [device(expert_at(k), j) for k in range(1, EXPERTS)]
    peers += [device(e, member_at(k)) for k in range(1, m)] + [core]
    barrier = pltpu.get_barrier_semaphore()
    for peer in peers:
        pl.semaphore_signal(barrier, inc=1, device_id=peer, device_id_type=MESH)

    up_step, down_step = wu.shape[0] // PIECES, wd.shape[0] // PIECES

    def up_copy(i):
        part = pl.ds(i * up_step, up_step)
        return pltpu.make_async_copy(wu_hbm.at[part], wu.at[part], wu_sem.at[i])

    def down_copy(i):
        part = pl.ds(i * down_step, down_step)
        return pltpu.make_async_copy(wd_hbm.at[part], wd.at[part], wd_sem.at[i])

    for i in range(PIECES):
        up_copy(i).start()
    for i in range(PIECES):
        down_copy(i).start()

    kv_heads = nkv_ref.shape[1] // (2 * HEAD_DIM)
    group = half // (kv_heads * HEAD_DIM)
    cache_len = cache_ref.shape[2]
    scaling = HEAD_DIM ** (-0.5)
    shape = (group * rows, rows * cache_len)
    row_tok = lax.rem(lax.broadcasted_iota(jnp.int32, shape, 0), rows)
    col = lax.broadcasted_iota(jnp.int32, shape, 1)
    col_tok = lax.div(col, cache_len)
    col_pos = lax.rem(col, cache_len).astype(F32)
    lens = jnp.concatenate([meta_ref[:, 4:5]] * group, axis=0)
    visible = (row_tok == col_tok) & (col_pos < lens)
    for g in range(kv_heads):
        cols = pl.ds(g * HEAD_DIM, HEAD_DIM)
        heads = [pl.ds((g * group + i) * HEAD_DIM, HEAD_DIM) for i in range(group)]
        query = jnp.concatenate([q_ref[:, h] for h in heads], axis=0)
        keys = cache_ref[:, 0, :, cols].reshape(rows * cache_len, HEAD_DIM)
        values = cache_ref[:, 1, :, cols].reshape(rows * cache_len, HEAD_DIM)
        new_key = jnp.concatenate([nkv_ref[:, cols].astype(F32)] * group, axis=0)
        new_value = nkv_ref[:, pl.ds((kv_heads + g) * HEAD_DIM, HEAD_DIM)].astype(F32)
        new_value = jnp.concatenate([new_value] * group, axis=0)
        old = lax.dot_general(
            query, keys, (((1,), (1,)), ((), ())), preferred_element_type=F32
        ) * scaling
        old = jnp.where(visible, old, NEG_FILL)
        new = jnp.sum(query.astype(F32) * new_key, axis=1, keepdims=True) * scaling
        top = jnp.maximum(jnp.max(old, axis=1, keepdims=True), new)
        old_p = jnp.where(visible, jnp.exp(old - top), 0.0)
        new_p = jnp.exp(new - top)
        total = jnp.sum(old_p, axis=1, keepdims=True) + new_p
        old_w = (old_p / total).astype(BF16)
        new_w = (new_p / total).astype(BF16).astype(F32)
        attended = jnp.dot(old_w, values, preferred_element_type=F32) + new_w * new_value
        attended = attended.astype(BF16).astype(F32)
        for i, h in enumerate(heads):
            piece = attended[i * rows : (i + 1) * rows]
            x[c, j, e, :, h] = (res_ref[:, h].astype(F32) + piece).astype(BF16)

    pl.semaphore_wait(barrier, len(peers))

    def move(part, jj, ee, send, recv, peer):
        block = x.at[part, jj, ee]
        return pltpu.make_async_remote_copy(
            src_ref=block, dst_ref=block, send_sem=send, recv_sem=recv,
            device_id=peer, device_id_type=MESH,
        )

    def over_experts(k):
        return move(c, j, e, e_send.at[k], x_recv.at[0, j, e], device(expert_at(k), j))

    def over_members(k, i):
        ee = expert_at(i)
        return move(c, j, ee, m_send.at[k, i], x_recv.at[0, j, ee], device(e, member_at(k)))

    def over_cores(k, i):
        jj, ee = member_at(k), expert_at(i)
        return move(c, jj, ee, c_send.at[k, i], x_recv.at[1, jj, ee], core)

    def arrived(other, jj, ee):
        part = 1 - c if other else c
        move(part, jj, ee, e_send.at[0], x_recv.at[other, jj, ee], core).wait_recv()

    sent = []

    def start(copy):
        copy.start()
        sent.append(copy)

    for k in (2, 1, 3):
        start(over_experts(k))
    for i in (0, 1, 3, 2):
        if i:
            arrived(0, j, expert_at(i))
        for k in range(1, m):
            start(over_members(k, i))
        start(over_cores(0, i))

    order = [(0, i) for i in (0, 1, 3, 2)]
    later = [(k, i) for i in (0, 1, 3, 2) for k in range(1, m)]

    def normalize(k, i):
        jj, ee = member_at(k), expert_at(i)
        arrived(1, jj, ee)
        low = x[0, jj, ee].astype(F32)
        high = x[1, jj, ee].astype(F32)
        square = jnp.sum(low * low, axis=1, keepdims=True)
        square = square + jnp.sum(high * high, axis=1, keepdims=True)
        scale = lax.rsqrt(square / (2 * half) + EPSILON)
        normed[jj, ee, :, pl.ds(0, half)] = (
            low * scale * gain_ref[:, pl.ds(0, half)].astype(F32)
        ).astype(BF16)
        normed[jj, ee, :, pl.ds(half, half)] = (
            high * scale * gain_ref[:, pl.ds(half, half)].astype(F32)
        ).astype(BF16)

    for k, i in later:
        arrived(0, member_at(k), expert_at(i))
        start(over_cores(k, i))
        if order:
            normalize(*order.pop(0))
    for k, i in order + later:
        normalize(k, i)

    for i in range(PIECES):
        up_copy(i).wait()
    tokens = EXPERTS * m * rows
    step = 256

    @pl.loop(0, wu.shape[1] // step)
    def _(n):
        cols = pl.ds(pl.multiple_of(n * step, step), step)
        up = jnp.dot(
            normed[...].reshape(tokens, 2 * half), wu[:, cols], preferred_element_type=F32
        )
        hidden[:, cols] = (up / (1.0 + jnp.exp(-up))).astype(BF16)

    for i in range(PIECES):
        down_copy(i).wait()

    def project(part, n):
        cols = pl.ds(pl.multiple_of(part * half + n * width, 128), width)
        value = jnp.dot(hidden[...], wd[:, cols], preferred_element_type=F32)
        return value.reshape(m, EXPERTS, rows, width)

    def remote(src, dst, send, recv, peer):
        return pltpu.make_async_remote_copy(
            src_ref=src, dst_ref=dst, send_sem=send, recv_sem=recv,
            device_id=peer, device_id_type=MESH,
        )

    def core_copy(n):
        return remote(core_out.at[n], core_in.at[n], co_send.at[n], co_recv.at[n], core)

    def member_copy(n, k):
        jj = member_at(k)
        return remote(
            mem_out.at[n, jj], mem_in.at[n, j], mo_send.at[n, k], mo_recv.at[n, j], device(e, jj)
        )

    def member_arrived(n, k):
        jj = member_at(k)
        remote(
            mem_out.at[n, jj], mem_in.at[n, jj], mo_send.at[n, k], mo_recv.at[n, jj], device(e, jj)
        ).wait_recv()
        return mem_in[n, jj].astype(F32)

    def expert_copy(n, k):
        ee = expert_at(k)
        return remote(
            exp_out.at[n, ee], exp_in.at[n, e], eo_send.at[n, k], eo_recv.at[n, e], device(ee, j)
        )

    def expert_arrived(n, k):
        ee = expert_at(k)
        remote(
            exp_out.at[n, ee], exp_in.at[n, ee], eo_send.at[n, k], eo_recv.at[n, ee], device(ee, j)
        ).wait_recv()
        return exp_in[n, ee].astype(F32)

    def compute(n):
        core_out[n] = project(1 - c, n).astype(BF16)
        start(core_copy(n))
        keep[n % 2] = project(c, n)

    def sum_cores(n):
        core_copy(n).wait_recv()
        mem_out[n] = (keep[n % 2] + core_in[n].astype(F32)).astype(BF16)
        for k in range(1, m):
            start(member_copy(n, k))

    def sum_members(n):
        total = mem_out[n, j].astype(F32)
        for k in range(1, m):
            total = total + member_arrived(n, k)
        exp_out[n] = total.astype(BF16)
        for k in (2, 1, 3):
            start(expert_copy(n, k))

    def weight(ee):
        ids = meta_ref[:, 0:2]
        return jnp.sum(
            jnp.where(ids == ee.astype(F32), meta_ref[:, 2:4], 0.0), axis=1, keepdims=True
        )

    def finish(n):
        cols = pl.ds(n * width, width)
        total = weight(e) * exp_out[n, e].astype(F32)
        for k in range(1, EXPERTS):
            total = total + weight(expert_at(k)) * expert_arrived(n, k)
        out_ref[:, cols] = (x[c, j, e, :, cols].astype(F32) + total).astype(BF16)

    for n in range(CHUNKS + 2):
        if n < CHUNKS:
            compute(n)
            sum_cores(n)
        if 1 <= n <= CHUNKS:
            sum_members(n - 1)
        if n >= CHUNKS:
            for i in (range(CHUNKS - 1) if n == CHUNKS else [CHUNKS - 1]):
                finish(i)
    for copy in sent:
        copy.wait_send()


def local(
    queries, new_kv, cache_kv, lengths, residual, norm_gain, expert_ids, route_weights, w_up, w_down
):
    rows, half = queries.shape
    attn = lax.axis_size("attn")
    m = attn // EXPERTS
    width = half // CHUNKS
    meta = jnp.concatenate(
        [expert_ids.astype(F32), route_weights.astype(F32), lengths.astype(F32)[:, None]], axis=1
    )
    vmem = pl.BlockSpec(memory_space=pltpu.VMEM)
    hbm = pl.BlockSpec(memory_space=pl.ANY)
    dma = pltpu.SemaphoreType.DMA
    tokens = attn * rows
    return pl.pallas_call(
        functools.partial(kernel, m),
        out_shape=jax.ShapeDtypeStruct((rows, half), BF16),
        in_specs=[vmem] * 6 + [hbm] * 2,
        out_specs=vmem,
        scratch_shapes=[
            pltpu.VMEM(w_up.shape, BF16),
            pltpu.VMEM(w_down.shape, BF16),
            pltpu.VMEM((2, m, EXPERTS, rows, half), BF16),
            pltpu.VMEM((m, EXPERTS, rows, 2 * half), BF16),
            pltpu.VMEM((tokens, w_up.shape[1]), BF16),
            pltpu.VMEM((CHUNKS, m, EXPERTS, rows, width), BF16),
            pltpu.VMEM((CHUNKS, m, EXPERTS, rows, width), BF16),
            pltpu.VMEM((2, m, EXPERTS, rows, width), F32),
            pltpu.VMEM((CHUNKS, m, EXPERTS, rows, width), BF16),
            pltpu.VMEM((CHUNKS, m, EXPERTS, rows, width), BF16),
            pltpu.VMEM((CHUNKS, EXPERTS, rows, width), BF16),
            pltpu.VMEM((CHUNKS, EXPERTS, rows, width), BF16),
            dma((PIECES,)),
            dma((PIECES,)),
            dma((2, m, EXPERTS)),
            dma((EXPERTS,)),
            dma((m, EXPERTS)),
            dma((m, EXPERTS)),
            dma((CHUNKS,)),
            dma((CHUNKS,)),
            dma((CHUNKS, m)),
            dma((CHUNKS, m)),
            dma((CHUNKS, EXPERTS)),
            dma((CHUNKS, EXPERTS)),

        ],
        compiler_params=pltpu.CompilerParams(
            collective_id=0, has_side_effects=True, vmem_limit_bytes=62 * 2**20
        ),
    )(
        queries, new_kv.reshape(rows, -1), cache_kv, residual, norm_gain.reshape(1, -1), meta,
        w_up, w_down,
    )


def solution(mesh):
    in_specs = (
        P(("group", "attn"), "expert"),
        P(("group", "attn"), None, "expert"),
        P(("group", "attn"), None, None, "expert"),
        P(("group", "attn")),
        P(("group", "attn"), "expert"),
        P(),
        P(("group", "attn"), None),
        P(("group", "attn"), None),
        P(None, ("attn", "expert")),
        P(("attn", "expert"), None),
    )
    out_specs = P(("group", "attn"), "expert")
    return jax.shard_map(local, mesh=mesh, in_specs=in_specs, out_specs=out_specs, check_vma=False)
```

```python
import functools

import jax
import jax.numpy as jnp
from jax import lax
from jax.experimental import pallas as pl
from jax.experimental.pallas import tpu as pltpu
from jax.sharding import PartitionSpec as P

HEAD_DIM = 128
EXPERTS = 4
EPSILON = 1e-05
NEG_FILL = -1e30
MESH = pl.DeviceIdType.MESH
CHUNKS = 2
PIECES = 8
F32 = jnp.float32
BF16 = jnp.bfloat16


def kernel(
    m, q_ref, nkv_ref, cache_ref, res_ref, gain_ref, len_ref, id_ref, route_ref, wu_hbm, wd_hbm, out_ref,
    wu, wd, x, normed, hidden, core_out, core_in, keep, mem_out, mem_in, exp_out, exp_in,
    wu_sem, wd_sem, x_recv, e_send, m_send, c_send,
    co_send, co_recv, mo_send, mo_recv, eo_send, eo_recv,
):
    a = lax.axis_index("attn")
    c = lax.axis_index("expert")
    e = lax.div(a, m)
    j = lax.rem(a, m)
    core = {"attn": a, "expert": 1 - c}
    rows, half = q_ref.shape
    width = half // CHUNKS

    def expert_at(k):
        return lax.rem(e + k, EXPERTS)

    def member_at(k):
        return lax.rem(j + k, m)

    def device(ee, jj):
        return {"attn": ee * m + jj, "expert": c}

    peers = [device(expert_at(k), j) for k in range(1, EXPERTS)]
    peers += [device(e, member_at(k)) for k in range(1, m)] + [core]
    barrier = pltpu.get_barrier_semaphore()
    for peer in peers:
        pl.semaphore_signal(barrier, inc=1, device_id=peer, device_id_type=MESH)

    up_step, down_step = wu.shape[0] // PIECES, wd.shape[0] // PIECES

    def up_copy(i):
        part = pl.ds(i * up_step, up_step)
        return pltpu.make_async_copy(wu_hbm.at[part], wu.at[part], wu_sem.at[i])

    def down_copy(i):
        part = pl.ds(i * down_step, down_step)
        return pltpu.make_async_copy(wd_hbm.at[part], wd.at[part], wd_sem.at[i])

    for i in range(PIECES):
        up_copy(i).start()
    for i in range(PIECES):
        down_copy(i).start()

    kv_heads = nkv_ref.shape[2] // HEAD_DIM
    group = half // (kv_heads * HEAD_DIM)
    cache_len = cache_ref.shape[2]
    scaling = HEAD_DIM ** (-0.5)
    shape = (group * rows, rows * cache_len)
    row_tok = lax.rem(lax.broadcasted_iota(jnp.int32, shape, 0), rows)
    col = lax.broadcasted_iota(jnp.int32, shape, 1)
    col_tok = lax.div(col, cache_len)
    col_pos = lax.rem(col, cache_len)
    lens = jnp.concatenate([len_ref[...]] * group, axis=0)
    visible = (row_tok == col_tok) & (col_pos < lens)
    for g in range(kv_heads):
        cols = pl.ds(g * HEAD_DIM, HEAD_DIM)
        heads = [pl.ds((g * group + i) * HEAD_DIM, HEAD_DIM) for i in range(group)]
        query = jnp.concatenate([q_ref[:, h] for h in heads], axis=0)
        keys = cache_ref[:, 0, :, cols].reshape(rows * cache_len, HEAD_DIM)
        values = cache_ref[:, 1, :, cols].reshape(rows * cache_len, HEAD_DIM)
        new_key = jnp.concatenate([nkv_ref[:, 0, cols].astype(F32)] * group, axis=0)
        new_value = nkv_ref[:, 1, cols].astype(F32)
        new_value = jnp.concatenate([new_value] * group, axis=0)
        old = lax.dot_general(
            query, keys, (((1,), (1,)), ((), ())), preferred_element_type=F32
        ) * scaling
        old = jnp.where(visible, old, NEG_FILL)
        new = jnp.sum(query.astype(F32) * new_key, axis=1, keepdims=True) * scaling
        top = jnp.maximum(jnp.max(old, axis=1, keepdims=True), new)
        old_p = jnp.where(visible, jnp.exp(old - top), 0.0)
        new_p = jnp.exp(new - top)
        total = jnp.sum(old_p, axis=1, keepdims=True) + new_p
        old_w = (old_p / total).astype(BF16)
        new_w = (new_p / total).astype(BF16).astype(F32)
        attended = jnp.dot(old_w, values, preferred_element_type=F32) + new_w * new_value
        attended = attended.astype(BF16).astype(F32)
        for i, h in enumerate(heads):
            piece = attended[i * rows : (i + 1) * rows]
            x[c, j, e, :, h] = (res_ref[:, h].astype(F32) + piece).astype(BF16)

    pl.semaphore_wait(barrier, len(peers))

    def move(part, jj, ee, send, recv, peer):
        block = x.at[part, jj, ee]
        return pltpu.make_async_remote_copy(
            src_ref=block, dst_ref=block, send_sem=send, recv_sem=recv,
            device_id=peer, device_id_type=MESH,
        )

    def over_experts(k):
        return move(c, j, e, e_send.at[k], x_recv.at[0, j, e], device(expert_at(k), j))

    def over_members(k, i):
        ee = expert_at(i)
        return move(c, j, ee, m_send.at[k, i], x_recv.at[0, j, ee], device(e, member_at(k)))

    def over_cores(k, i):
        jj, ee = member_at(k), expert_at(i)
        return move(c, jj, ee, c_send.at[k, i], x_recv.at[1, jj, ee], core)

    def arrived(other, jj, ee):
        part = 1 - c if other else c
        move(part, jj, ee, e_send.at[0], x_recv.at[other, jj, ee], core).wait_recv()

    sent = []

    def start(copy):
        copy.start()
        sent.append(copy)

    for k in (2, 1, 3):
        start(over_experts(k))
    for i in (0, 1, 3, 2):
        if i:
            arrived(0, j, expert_at(i))
        for k in range(1, m):
            start(over_members(k, i))
        start(over_cores(0, i))

    order = [(0, i) for i in (0, 1, 3, 2)]
    later = [(k, i) for i in (0, 1, 3, 2) for k in range(1, m)]

    def normalize(k, i):
        jj, ee = member_at(k), expert_at(i)
        arrived(1, jj, ee)
        low = x[0, jj, ee].astype(F32)
        high = x[1, jj, ee].astype(F32)
        square = jnp.sum(low * low, axis=1, keepdims=True)
        square = square + jnp.sum(high * high, axis=1, keepdims=True)
        scale = lax.rsqrt(square / (2 * half) + EPSILON)
        normed[jj, ee, :, pl.ds(0, half)] = (
            low * scale * gain_ref[pl.ds(0, half)].reshape(1, half).astype(F32)
        ).astype(BF16)
        normed[jj, ee, :, pl.ds(half, half)] = (
            high * scale * gain_ref[pl.ds(half, half)].reshape(1, half).astype(F32)
        ).astype(BF16)

    for k, i in later:
        arrived(0, member_at(k), expert_at(i))
        start(over_cores(k, i))
        if order:
            normalize(*order.pop(0))
    for k, i in order + later:
        normalize(k, i)

    for i in range(PIECES):
        up_copy(i).wait()
    tokens = EXPERTS * m * rows
    step = 256

    @pl.loop(0, wu.shape[1] // step)
    def _(n):
        cols = pl.ds(pl.multiple_of(n * step, step), step)
        up = jnp.dot(
            normed[...].reshape(tokens, 2 * half), wu[:, cols], preferred_element_type=F32
        )
        hidden[:, cols] = (up / (1.0 + jnp.exp(-up))).astype(BF16)

    for i in range(PIECES):
        down_copy(i).wait()

    def project(part, n):
        cols = pl.ds(pl.multiple_of(part * half + n * width, 128), width)
        value = jnp.dot(hidden[...], wd[:, cols], preferred_element_type=F32)
        return value.reshape(m, EXPERTS, rows, width)

    def remote(src, dst, send, recv, peer):
        return pltpu.make_async_remote_copy(
            src_ref=src, dst_ref=dst, send_sem=send, recv_sem=recv,
            device_id=peer, device_id_type=MESH,
        )

    def core_copy(n):
        return remote(core_out.at[n], core_in.at[n], co_send.at[n], co_recv.at[n], core)

    def member_copy(n, k):
        jj = member_at(k)
        return remote(
            mem_out.at[n, jj], mem_in.at[n, j], mo_send.at[n, k], mo_recv.at[n, j], device(e, jj)
        )

    def member_arrived(n, k):
        jj = member_at(k)
        remote(
            mem_out.at[n, jj], mem_in.at[n, jj], mo_send.at[n, k], mo_recv.at[n, jj], device(e, jj)
        ).wait_recv()
        return mem_in[n, jj].astype(F32)

    def expert_copy(n, k):
        ee = expert_at(k)
        return remote(
            exp_out.at[n, ee], exp_in.at[n, e], eo_send.at[n, k], eo_recv.at[n, e], device(ee, j)
        )

    def expert_arrived(n, k):
        ee = expert_at(k)
        remote(
            exp_out.at[n, ee], exp_in.at[n, ee], eo_send.at[n, k], eo_recv.at[n, ee], device(ee, j)
        ).wait_recv()
        return exp_in[n, ee].astype(F32)

    def compute(n):
        core_out[n] = project(1 - c, n).astype(BF16)
        start(core_copy(n))
        keep[n % 2] = project(c, n)

    def sum_cores(n):
        core_copy(n).wait_recv()
        mem_out[n] = (keep[n % 2] + core_in[n].astype(F32)).astype(BF16)
        for k in range(1, m):
            start(member_copy(n, k))

    def sum_members(n):
        total = mem_out[n, j].astype(F32)
        for k in range(1, m):
            total = total + member_arrived(n, k)
        exp_out[n] = total.astype(BF16)
        for k in (2, 1, 3):
            start(expert_copy(n, k))

    def weight(ee):
        routed = jnp.where(id_ref[...] == ee, route_ref[...].astype(F32), 0.0)
        return jnp.sum(routed, axis=1, keepdims=True)

    def finish(n):
        cols = pl.ds(n * width, width)
        total = weight(e) * exp_out[n, e].astype(F32)
        for k in range(1, EXPERTS):
            total = total + weight(expert_at(k)) * expert_arrived(n, k)
        out_ref[:, cols] = (x[c, j, e, :, cols].astype(F32) + total).astype(BF16)

    for n in range(CHUNKS + 2):
        if n < CHUNKS:
            compute(n)
            sum_cores(n)
        if 1 <= n <= CHUNKS:
            sum_members(n - 1)
        if n >= CHUNKS:
            for i in (range(CHUNKS - 1) if n == CHUNKS else [CHUNKS - 1]):
                finish(i)
    for copy in sent:
        copy.wait_send()


def local(
    queries, new_kv, cache_kv, lengths, residual, norm_gain, expert_ids, route_weights, w_up, w_down
):
    rows, half = queries.shape
    attn = lax.axis_size("attn")
    m = attn // EXPERTS
    width = half // CHUNKS
    vmem = pl.BlockSpec(memory_space=pltpu.VMEM)
    hbm = pl.BlockSpec(memory_space=pl.ANY)
    dma = pltpu.SemaphoreType.DMA
    tokens = attn * rows
    return pl.pallas_call(
        functools.partial(kernel, m),
        out_shape=jax.ShapeDtypeStruct((rows, half), BF16),
        in_specs=[vmem] * 8 + [hbm] * 2,
        out_specs=vmem,
        scratch_shapes=[
            pltpu.VMEM(w_up.shape, BF16),
            pltpu.VMEM(w_down.shape, BF16),
            pltpu.VMEM((2, m, EXPERTS, rows, half), BF16),
            pltpu.VMEM((m, EXPERTS, rows, 2 * half), BF16),
            pltpu.VMEM((tokens, w_up.shape[1]), BF16),
            pltpu.VMEM((CHUNKS, m, EXPERTS, rows, width), BF16),
            pltpu.VMEM((CHUNKS, m, EXPERTS, rows, width), BF16),
            pltpu.VMEM((2, m, EXPERTS, rows, width), F32),
            pltpu.VMEM((CHUNKS, m, EXPERTS, rows, width), BF16),
            pltpu.VMEM((CHUNKS, m, EXPERTS, rows, width), BF16),
            pltpu.VMEM((CHUNKS, EXPERTS, rows, width), BF16),
            pltpu.VMEM((CHUNKS, EXPERTS, rows, width), BF16),
            dma((PIECES,)),
            dma((PIECES,)),
            dma((2, m, EXPERTS)),
            dma((EXPERTS,)),
            dma((m, EXPERTS)),
            dma((m, EXPERTS)),
            dma((CHUNKS,)),
            dma((CHUNKS,)),
            dma((CHUNKS, m)),
            dma((CHUNKS, m)),
            dma((CHUNKS, EXPERTS)),
            dma((CHUNKS, EXPERTS)),

        ],
        compiler_params=pltpu.CompilerParams(
            collective_id=0, has_side_effects=True, vmem_limit_bytes=62 * 2**20
        ),
    )(
        queries, new_kv, cache_kv, residual, norm_gain, lengths[:, None], expert_ids, route_weights,
        w_up, w_down,
    )


def solution(mesh):
    in_specs = (
        P(("group", "attn"), "expert"),
        P(("group", "attn"), None, "expert"),
        P(("group", "attn"), None, None, "expert"),
        P(("group", "attn")),
        P(("group", "attn"), "expert"),
        P(),
        P(("group", "attn"), None),
        P(("group", "attn"), None),
        P(None, ("attn", "expert")),
        P(("attn", "expert"), None),
    )
    out_specs = P(("group", "attn"), "expert")
    return jax.shard_map(local, mesh=mesh, in_specs=in_specs, out_specs=out_specs, check_vma=False)
```

```python
import functools

import jax
import jax.numpy as jnp
from jax import lax
from jax.experimental import pallas as pl
from jax.experimental.pallas import tpu as pltpu
from jax.sharding import PartitionSpec as P

HEAD_DIM = 128
EXPERTS = 4
EPSILON = 1e-05
NEG_FILL = -1e30
MESH = pl.DeviceIdType.MESH
CHUNKS = 2
PIECES = 8
F32 = jnp.float32
BF16 = jnp.bfloat16


def kernel(
    m, q_ref, nkv_ref, cache_ref, res_ref, gain_ref, len_ref, id_ref, route_ref, wu_hbm, wd_hbm, out_ref,
    wu, wd, x, normed, hidden, core_out, core_in, keep, mem_out, mem_in, exp_out, exp_in,
    wu_sem, wd_sem, x_recv, e_send, m_send, c_send,
    co_send, co_recv, mo_send, mo_recv, eo_send, eo_recv,
):
    a = lax.axis_index("attn")
    c = lax.axis_index("expert")
    e = lax.div(a, m)
    j = lax.rem(a, m)
    core = {"attn": a, "expert": 1 - c}
    rows, half = q_ref.shape
    width = half // CHUNKS

    def expert_at(k):
        return lax.rem(e + k, EXPERTS)

    def member_at(k):
        return lax.rem(j + k, m)

    def device(ee, jj):
        return {"attn": ee * m + jj, "expert": c}

    peers = [device(expert_at(k), j) for k in range(1, EXPERTS)]
    peers += [device(e, member_at(k)) for k in range(1, m)] + [core]
    barrier = pltpu.get_barrier_semaphore()
    for peer in peers:
        pl.semaphore_signal(barrier, inc=1, device_id=peer, device_id_type=MESH)

    up_step, down_step = wu.shape[0] // PIECES, wd.shape[0] // PIECES

    def up_copy(i):
        part = pl.ds(i * up_step, up_step)
        return pltpu.make_async_copy(wu_hbm.at[part], wu.at[part], wu_sem.at[i])

    def down_copy(i):
        part = pl.ds(i * down_step, down_step)
        return pltpu.make_async_copy(wd_hbm.at[part], wd.at[part], wd_sem.at[i])

    for i in range(PIECES):
        up_copy(i).start()
    for i in range(PIECES):
        down_copy(i).start()

    kv_heads = nkv_ref.shape[2] // HEAD_DIM
    group = half // (kv_heads * HEAD_DIM)
    cache_len = cache_ref.shape[2]
    scaling = HEAD_DIM ** (-0.5)
    shape = (group * rows, rows * cache_len)
    row_tok = lax.rem(lax.broadcasted_iota(jnp.int32, shape, 0), rows)
    col = lax.broadcasted_iota(jnp.int32, shape, 1)
    col_tok = lax.div(col, cache_len)
    col_pos = lax.rem(col, cache_len)
    lens = jnp.concatenate([len_ref[...]] * group, axis=0)
    visible = (row_tok == col_tok) & (col_pos < lens)
    for g in range(kv_heads):
        cols = pl.ds(g * HEAD_DIM, HEAD_DIM)
        heads = [pl.ds((g * group + i) * HEAD_DIM, HEAD_DIM) for i in range(group)]
        query = jnp.concatenate([q_ref[:, h] for h in heads], axis=0)
        keys = cache_ref[:, 0, :, cols].reshape(rows * cache_len, HEAD_DIM)
        values = cache_ref[:, 1, :, cols].reshape(rows * cache_len, HEAD_DIM)
        new_key = jnp.concatenate([nkv_ref[:, 0, cols].astype(F32)] * group, axis=0)
        new_value = nkv_ref[:, 1, cols].astype(F32)
        new_value = jnp.concatenate([new_value] * group, axis=0)
        old = lax.dot_general(
            query, keys, (((1,), (1,)), ((), ())), preferred_element_type=F32
        ) * scaling
        old = jnp.where(visible, old, NEG_FILL)
        new = jnp.sum(query.astype(F32) * new_key, axis=1, keepdims=True) * scaling
        top = jnp.maximum(jnp.max(old, axis=1, keepdims=True), new)
        old_p = jnp.where(visible, jnp.exp(old - top), 0.0)
        new_p = jnp.exp(new - top)
        total = jnp.sum(old_p, axis=1, keepdims=True) + new_p
        old_w = (old_p / total).astype(BF16)
        new_w = (new_p / total).astype(BF16).astype(F32)
        attended = jnp.dot(old_w, values, preferred_element_type=F32) + new_w * new_value
        attended = attended.astype(BF16).astype(F32)
        for i, h in enumerate(heads):
            piece = attended[i * rows : (i + 1) * rows]
            x[c, j, e, :, h] = (res_ref[:, h].astype(F32) + piece).astype(BF16)

    pl.semaphore_wait(barrier, len(peers))

    def move(part, jj, ee, send, recv, peer):
        block = x.at[part, jj, ee]
        return pltpu.make_async_remote_copy(
            src_ref=block, dst_ref=block, send_sem=send, recv_sem=recv,
            device_id=peer, device_id_type=MESH,
        )

    def over_experts(k):
        return move(c, j, e, e_send.at[k], x_recv.at[0, j, e], device(expert_at(k), j))

    def over_members(k, i):
        ee = expert_at(i)
        return move(c, j, ee, m_send.at[k, i], x_recv.at[0, j, ee], device(e, member_at(k)))

    def over_cores(k, i):
        jj, ee = member_at(k), expert_at(i)
        return move(c, jj, ee, c_send.at[k, i], x_recv.at[1, jj, ee], core)

    def arrived(other, jj, ee):
        part = 1 - c if other else c
        move(part, jj, ee, e_send.at[0], x_recv.at[other, jj, ee], core).wait_recv()

    sent = []

    def start(copy):
        copy.start()
        sent.append(copy)

    for k in (1, 3, 2):
        start(over_experts(k))
    for i in (0, 1, 3, 2):
        if i:
            arrived(0, j, expert_at(i))
        for k in range(1, m):
            start(over_members(k, i))
        start(over_cores(0, i))

    order = [(0, i) for i in (0, 1, 3, 2)]
    later = [(k, i) for i in (0, 1, 3, 2) for k in range(1, m)]

    def normalize(k, i):
        jj, ee = member_at(k), expert_at(i)
        arrived(1, jj, ee)
        low = x[0, jj, ee].astype(F32)
        high = x[1, jj, ee].astype(F32)
        square = jnp.sum(low * low, axis=1, keepdims=True)
        square = square + jnp.sum(high * high, axis=1, keepdims=True)
        scale = lax.rsqrt(square / (2 * half) + EPSILON)
        normed[jj, ee, :, pl.ds(0, half)] = (
            low * scale * gain_ref[pl.ds(0, half)].reshape(1, half).astype(F32)
        ).astype(BF16)
        normed[jj, ee, :, pl.ds(half, half)] = (
            high * scale * gain_ref[pl.ds(half, half)].reshape(1, half).astype(F32)
        ).astype(BF16)

    for k, i in later:
        arrived(0, member_at(k), expert_at(i))
        start(over_cores(k, i))
        if order:
            normalize(*order.pop(0))
    for k, i in order + later:
        normalize(k, i)

    for i in range(PIECES):
        up_copy(i).wait()
    tokens = EXPERTS * m * rows
    step = 256

    @pl.loop(0, wu.shape[1] // step)
    def _(n):
        cols = pl.ds(pl.multiple_of(n * step, step), step)
        up = jnp.dot(
            normed[...].reshape(tokens, 2 * half), wu[:, cols], preferred_element_type=F32
        )
        hidden[:, cols] = (up / (1.0 + jnp.exp(-up))).astype(BF16)

    for i in range(PIECES):
        down_copy(i).wait()

    def project(part, n):
        cols = pl.ds(pl.multiple_of(part * half + n * width, 128), width)
        value = jnp.dot(hidden[...], wd[:, cols], preferred_element_type=F32)
        return value.reshape(m, EXPERTS, rows, width)

    def remote(src, dst, send, recv, peer):
        return pltpu.make_async_remote_copy(
            src_ref=src, dst_ref=dst, send_sem=send, recv_sem=recv,
            device_id=peer, device_id_type=MESH,
        )

    def core_copy(n):
        return remote(core_out.at[n], core_in.at[n], co_send.at[n], co_recv.at[n], core)

    def member_copy(n, k):
        jj = member_at(k)
        return remote(
            mem_out.at[n, jj], mem_in.at[n, j], mo_send.at[n, k], mo_recv.at[n, j], device(e, jj)
        )

    def member_arrived(n, k):
        jj = member_at(k)
        remote(
            mem_out.at[n, jj], mem_in.at[n, jj], mo_send.at[n, k], mo_recv.at[n, jj], device(e, jj)
        ).wait_recv()
        return mem_in[n, jj].astype(F32)

    def expert_copy(n, k):
        ee = expert_at(k)
        return remote(
            exp_out.at[n, ee], exp_in.at[n, e], eo_send.at[n, k], eo_recv.at[n, e], device(ee, j)
        )

    def expert_arrived(n, k):
        ee = expert_at(k)
        remote(
            exp_out.at[n, ee], exp_in.at[n, ee], eo_send.at[n, k], eo_recv.at[n, ee], device(ee, j)
        ).wait_recv()
        return exp_in[n, ee].astype(F32)

    def compute(n):
        core_out[n] = project(1 - c, n).astype(BF16)
        start(core_copy(n))
        keep[n % 2] = project(c, n)

    def sum_cores(n):
        core_copy(n).wait_recv()
        mem_out[n] = (keep[n % 2] + core_in[n].astype(F32)).astype(BF16)
        for k in range(1, m):
            start(member_copy(n, k))

    def sum_members(n):
        total = mem_out[n, j].astype(F32)
        for k in range(1, m):
            total = total + member_arrived(n, k)
        exp_out[n] = total.astype(BF16)
        for k in (1, 3, 2):
            start(expert_copy(n, k))

    def weight(ee):
        routed = jnp.where(id_ref[...] == ee, route_ref[...].astype(F32), 0.0)
        return jnp.sum(routed, axis=1, keepdims=True)

    def finish(n):
        cols = pl.ds(n * width, width)
        total = weight(e) * exp_out[n, e].astype(F32)
        for k in range(1, EXPERTS):
            total = total + weight(expert_at(k)) * expert_arrived(n, k)
        out_ref[:, cols] = (x[c, j, e, :, cols].astype(F32) + total).astype(BF16)

    for n in range(CHUNKS + 2):
        if n < CHUNKS:
            compute(n)
            sum_cores(n)
        if 1 <= n <= CHUNKS:
            sum_members(n - 1)
        if n >= CHUNKS:
            for i in (range(CHUNKS - 1) if n == CHUNKS else [CHUNKS - 1]):
                finish(i)
    for copy in sent:
        copy.wait_send()


def local(
    queries, new_kv, cache_kv, lengths, residual, norm_gain, expert_ids, route_weights, w_up, w_down
):
    rows, half = queries.shape
    attn = lax.axis_size("attn")
    m = attn // EXPERTS
    width = half // CHUNKS
    vmem = pl.BlockSpec(memory_space=pltpu.VMEM)
    hbm = pl.BlockSpec(memory_space=pl.ANY)
    dma = pltpu.SemaphoreType.DMA
    tokens = attn * rows
    return pl.pallas_call(
        functools.partial(kernel, m),
        out_shape=jax.ShapeDtypeStruct((rows, half), BF16),
        in_specs=[vmem] * 8 + [hbm] * 2,
        out_specs=vmem,
        scratch_shapes=[
            pltpu.VMEM(w_up.shape, BF16),
            pltpu.VMEM(w_down.shape, BF16),
            pltpu.VMEM((2, m, EXPERTS, rows, half), BF16),
            pltpu.VMEM((m, EXPERTS, rows, 2 * half), BF16),
            pltpu.VMEM((tokens, w_up.shape[1]), BF16),
            pltpu.VMEM((CHUNKS, m, EXPERTS, rows, width), BF16),
            pltpu.VMEM((CHUNKS, m, EXPERTS, rows, width), BF16),
            pltpu.VMEM((2, m, EXPERTS, rows, width), F32),
            pltpu.VMEM((CHUNKS, m, EXPERTS, rows, width), BF16),
            pltpu.VMEM((CHUNKS, m, EXPERTS, rows, width), BF16),
            pltpu.VMEM((CHUNKS, EXPERTS, rows, width), BF16),
            pltpu.VMEM((CHUNKS, EXPERTS, rows, width), BF16),
            dma((PIECES,)),
            dma((PIECES,)),
            dma((2, m, EXPERTS)),
            dma((EXPERTS,)),
            dma((m, EXPERTS)),
            dma((m, EXPERTS)),
            dma((CHUNKS,)),
            dma((CHUNKS,)),
            dma((CHUNKS, m)),
            dma((CHUNKS, m)),
            dma((CHUNKS, EXPERTS)),
            dma((CHUNKS, EXPERTS)),

        ],
        compiler_params=pltpu.CompilerParams(
            collective_id=0, has_side_effects=True, vmem_limit_bytes=62 * 2**20
        ),
    )(
        queries, new_kv, cache_kv, residual, norm_gain, lengths[:, None], expert_ids, route_weights,
        w_up, w_down,
    )


def solution(mesh):
    in_specs = (
        P(("group", "attn"), "expert"),
        P(("group", "attn"), None, "expert"),
        P(("group", "attn"), None, None, "expert"),
        P(("group", "attn")),
        P(("group", "attn"), "expert"),
        P(),
        P(("group", "attn"), None),
        P(("group", "attn"), None),
        P(None, ("attn", "expert")),
        P(("attn", "expert"), None),
    )
    out_specs = P(("group", "attn"), "expert")
    return jax.shard_map(local, mesh=mesh, in_specs=in_specs, out_specs=out_specs, check_vma=False)
```
